32 devices in a mesh: fib: 4 (over y, x), row: 4 (over z), slab: 2 (over core).
Axes of the slice: x: 2, y: 2, z: 4, core: 2. Of those that a mesh axis runs over, the one named last changes fastest.
Arguments:
- tensor: float32 [128, 128, 64, 128], P('fib', 'row', 'slab'), may hold values from -300 to 300
- factor_one: float32 [128, 64], replicated, may hold values from -0.5 to 0.5
- factor_two: float32 [128, 64], P('row'), may hold values from -50 to 50
- factor_three: float32 [64, 64], P('slab'), may hold values from -50 to 50
- factor_four: float32 [128, 64], replicated, may hold values from -0.5 to 0.5
Outputs:
- updated_factor: float32 [128, 64], replicated
- core_tensor: float32 [64, 64, 64, 64], P(None, ('row', 'slab'), 'fib')
The draws below stay inside these ranges and needn't reach their ends.
All inputs are finite; a program needn't handle non-finite values.
Results may differ from the reference program's by a relative error of at most 0.00015.
Values sent between devices are 32-bit elements; how exact they have to be, the bound alone decides.
No kernel may reach another device: no remote copies, remote signals or barrier semaphores. Data moves between devices by JAX's collectives and lax.ppermute only.
A program may use at most 256 MiB of HBM per device.

```python
import math
import jax
import jax.numpy as jnp
from jax import lax

R = 64
B1 = 32
I4 = 128
I1 = 128
I2 = 128
I3 = 64
N_FIB = 4


def rising_factor(key, length, columns, steep):
    noise = jnp.clip(jax.random.normal(key, (length, columns), jnp.float32), -4.0, 4.0)
    position = jnp.arange(columns, dtype=jnp.float32) / (columns - 1)
    wobble = jnp.exp(jax.random.uniform(jax.random.fold_in(key, 1), (columns,), jnp.float32, -0.3, 0.3))
    return noise * (steep ** position * wobble)[None, :] / math.sqrt(length)


def draw_factor_two(key, part):
    key = jax.random.fold_in(key, 2)
    steep = 3.0
    return rising_factor(key, I2, R, steep)


def draw_factor_three(key, part):
    key = jax.random.fold_in(key, 3)
    steep = 3.0
    return rising_factor(key, I3, R, steep)


def draw_tensor(key, part):
    key = jax.random.fold_in(key, 5)
    keys = jax.random.split(key, 4)
    shape = (I1, I2, I3, I4)
    rough = jnp.clip(jax.random.normal(keys[0], shape, jnp.float32), -4.0, 4.0)
    mixing = 0.3
    widest = 3.0
    common = jnp.clip(jax.random.normal(keys[1], (3, I2, I3, I4), jnp.float32), -4.0, 4.0)
    loadings = jax.random.uniform(keys[2], (I1, 3), jnp.float32, -1.0, 1.0)
    scales = jnp.exp(jax.random.uniform(keys[3], (I1,), jnp.float32, 0.0, math.log(widest)))
    shared = loadings[:, 0, None, None, None] * common[0][None]
    shared = shared + loadings[:, 1, None, None, None] * common[1][None]
    shared = shared + loadings[:, 2, None, None, None] * common[2][None]
    return scales[:, None, None, None] * (rough + mixing * shared)


def bell_draw(own_key, extent, width, bound, kind=jnp.bfloat16):
    values = width * jax.random.normal(own_key, extent, jnp.float32)
    return jnp.clip(values, min=-bound, max=bound).astype(kind)


def setup_inputs(seed: int = 0) -> dict:
    splits = jax.random.split(jax.random.key(seed), 6)
    tensor = draw_tensor(jax.random.fold_in(splits[5], 71), 0)
    factor_one = bell_draw(splits[1], (I1, R), I1 ** -0.5, 0.5, jnp.float32)
    factor_two = draw_factor_two(jax.random.fold_in(splits[5], 71), 0)
    factor_three = draw_factor_three(jax.random.fold_in(splits[5], 71), 0)
    factor_four = bell_draw(splits[4], (I4, R), I4 ** -0.5, 0.5, jnp.float32)
    return {"tensor": tensor, "factor_one": factor_one, "factor_two": factor_two, "factor_three": factor_three, "factor_four": factor_four}


def contract_block(block, factor_two, factor_three, factor_four):
    highest = lax.Precision.HIGHEST
    partial_four = jnp.einsum('ijkl,lr->ijkr', block, factor_four, precision=highest)
    partial_two = jnp.einsum('ijkr,jq->iqkr', partial_four, factor_two, precision=highest)
    return jnp.einsum('iqkr,kp->iqpr', partial_two, factor_three, precision=highest)

def orthonormal(target):
    highest = lax.Precision.HIGHEST
    result = target
    for repeat in range(2):
        crossed = jnp.dot(result.T, result, precision=highest)
        cholesky_factor = jnp.linalg.cholesky(crossed)
        result = jax.scipy.linalg.solve_triangular(cholesky_factor, result.T, lower=True).T
    return result

def reference(tensor, factor_one, factor_two, factor_three, factor_four):
    highest = lax.Precision.HIGHEST
    blocks = tensor.reshape(N_FIB, B1, I2, I3, I4)
    projected = lax.map(lambda piece: contract_block(piece, factor_two, factor_three, factor_four), blocks)
    unfolded = projected.reshape(I1, R * R * R)
    gram = jnp.dot(unfolded, unfolded.T, precision=highest)
    target = jnp.dot(gram, factor_one, precision=highest)
    updated = orthonormal(target)
    core = jnp.dot(updated.T, unfolded, precision=highest).reshape(R, R, R, R)
    return (updated, core)
```

```python
import functools
import itertools

import jax
import jax.numpy as jnp
from jax import lax
from jax.experimental import pallas as pl
from jax.experimental.pallas import tpu as pltpu
from jax.sharding import PartitionSpec as P

F32 = jnp.float32
BF16 = jnp.bfloat16
HIGHEST = lax.Precision.HIGHEST
LANES = 128
TILE = 8
NT = (((1,), (1,)), ((), ()))
NN = (((1,), (0,)), ((), ()))


def split(x):
    high = x.astype(BF16)
    return high, (x - high.astype(F32)).astype(BF16)


def split_outside(x):
    high = lax.reduce_precision(x, 8, 7)
    return high.astype(BF16), (x - high).astype(BF16)


def dot(a, b, dims=NN):
    return lax.dot_general(a, b, dims, preferred_element_type=F32)


def relative(x, axis, count, me):
    shape = x.shape
    width = 1
    while width < count:
        cut = shape[:axis] + (count // (2 * width), 2, shape[axis] // count * width) + shape[axis + 1:]
        y = x.reshape(cut)
        x = jnp.where((me // width) % 2 == 1, jnp.flip(y, axis + 1), y).reshape(shape)
        width *= 2
    return x


def partner(x, axes, count, distance):
    return lax.ppermute(x, axes, [(s, s ^ distance) for s in range(count)])


def in_hbm(x):
    return pltpu.with_memory_space_constraint(x, pltpu.HBM)


def gathered(x, axes, count):
    return [x] + [partner(x, axes, count, b) for b in range(1, count)]


def tree_sum(parts):
    while len(parts) > 1:
        parts = [a + b for a, b in zip(parts[::2], parts[1::2])]
    return parts[0]


def params(steps, megabytes=12):
    return pltpu.CompilerParams(
        dimension_semantics=("arbitrary",) * steps, vmem_limit_bytes=megabytes * 2 ** 20
    )


def contract_four(tensor, factor, me, first, chunk, parts, after):
    _, jl, kl, depth = tensor.shape
    ranks = factor.shape[1]
    m = LANES // jl
    groups = kl // m
    own = ranks // parts
    per = own // m

    def kernel(me_ref, x_ref, f_ref, *refs):
        outs, w_ref, s_ref = refs[len(after):-2], refs[-2], refs[-1]

        @pl.when(pl.program_id(0) == 0)
        def _():
            high, low = split(f_ref[...].T)
            w_ref[...] = jnp.concatenate(
                [jnp.concatenate([high, high], 1), jnp.concatenate([low, jnp.zeros_like(low)], 1)], 0)

        lane = lax.broadcasted_iota(jnp.int32, (1, 1, LANES), 2)
        weights = w_ref[...]
        for group in range(groups):
            rows = jnp.concatenate([x_ref[0, :, q * groups + group, :] for q in range(m)], axis=0)
            high, low = split(rows)
            found = dot(weights, jnp.concatenate([high, low], axis=1), NT)
            s_ref[:, group, :] = found[:ranks] + found[ranks:]
        for part in range(parts):
            mine = s_ref[pl.ds((me_ref[0] ^ part) * own, own)].reshape(per, m, groups, LANES)
            blocks = [mine[:, q] for q in range(m)]
            width = m // 2
            while width:
                upper = (lane // (jl * width)) % 2 == 1
                shift = jl * width
                for q in range(m):
                    if q & width == 0:
                        a, b = blocks[q], blocks[q + width]
                        blocks[q] = jnp.where(upper, pltpu.roll(b, shift, 2), a)
                        blocks[q + width] = jnp.where(upper, b, pltpu.roll(a, LANES - shift, 2))
                width //= 2
            for q in range(m):
                outs[part][0, :, q * groups:(q + 1) * groups, :] = blocks[q]

    return pl.pallas_call(
        kernel,
        grid_spec=pltpu.PrefetchScalarGridSpec(
            num_scalar_prefetch=1,
            grid=(chunk,),
            in_specs=[
                pl.BlockSpec((1, jl, kl, depth), lambda i, me: (first + i, 0, 0, 0)),
                pl.BlockSpec(factor.shape, lambda i, me: (0, 0)),
            ] + [pl.BlockSpec(memory_space=pl.ANY)] * len(after),
            out_specs=[pl.BlockSpec((1, per, kl, LANES), lambda i, me: (i, 0, 0, 0))] * parts,
            scratch_shapes=[
                pltpu.VMEM((2 * ranks, 2 * depth), BF16), pltpu.VMEM((ranks, groups, LANES), F32)],
        ),
        out_shape=[jax.ShapeDtypeStruct((chunk, per, kl, LANES), F32)] * parts,
        compiler_params=params(1),
        cost_estimate=pl.CostEstimate(
            flops=12 * chunk * jl * kl * depth * ranks, bytes_accessed=6 * chunk * jl * kl * depth, transcendentals=0
        ),
        name="mode_four",
    )(me, tensor, factor, *after)


def spread(pieces, m):
    jl, ranks = pieces[0].shape
    rows, wide = len(pieces) * m * jl, m * ranks

    def kernel(*refs):
        out_ref = refs[-1]
        out_ref[...] = jnp.zeros_like(out_ref)
        for n, ref in enumerate(refs[:-1]):
            for half, value in enumerate(split(ref[...])):
                for r in range(m):
                    at = (n * m + r) * jl
                    out_ref[at:at + jl, half * wide + r * ranks:half * wide + (r + 1) * ranks] = value

    return pl.pallas_call(
        kernel,
        in_specs=[pl.BlockSpec(memory_space=pltpu.VMEM)] * len(pieces),
        out_specs=pl.BlockSpec(memory_space=pltpu.VMEM),
        out_shape=jax.ShapeDtypeStruct((rows, 2 * wide), BF16),
        compiler_params=params(0),
        name="spread",
    )(*pieces)


def contract_two_three(pieces, order, weights_two, weights_three, rows, slabs, targets, after):
    chunk, per, kl, _ = pieces[0].shape
    wide = weights_two.shape[1] // 2
    ranks = weights_three.shape[0]
    share = ranks // targets
    count = len(pieces)

    def kernel(*refs):
        ins, two_ref, three_ref, outs = refs[:count], refs[count], refs[count + 1], refs[count + 2 + len(after):]
        taken = []
        for slab in range(slabs):
            taken.append(jnp.concatenate(
                [ins[order.index(row * slabs + slab)][...].reshape(chunk * kl, LANES) for row in range(rows)], axis=1))
        high, low = split(jnp.concatenate(taken, axis=0))
        two_high, two_low = two_ref[:, :wide], two_ref[:, wide:]
        half = dot(high, two_high) + dot(low, two_high) + dot(high, two_low)
        high, low = split(half)
        for i in range(chunk):
            spots = [slice((slab * chunk + i) * kl, (slab * chunk + i + 1) * kl) for slab in range(slabs)]
            own_high = jnp.concatenate([high[s] for s in spots], axis=0)
            own_low = jnp.concatenate([low[s] for s in spots], axis=0)
            full = dot(three_ref[...], jnp.concatenate([own_high, own_low, own_high], axis=0))
            for target in range(targets):
                outs[target][0, :, i, :] = full[target * share:(target + 1) * share]

    return pl.pallas_call(
        kernel,
        grid=(per,),
        in_specs=[pl.BlockSpec((chunk, 1, kl, LANES), lambda g: (0, g, 0, 0))] * count
        + [
            pl.BlockSpec(weights_two.shape, lambda g: (0, 0)),
            pl.BlockSpec(weights_three.shape, lambda g: (0, 0)),
        ] + [pl.BlockSpec(memory_space=pl.ANY)] * len(after),
        out_specs=[pl.BlockSpec((1, share, chunk, wide), lambda g: (g, 0, 0, 0))] * targets,
        out_shape=[jax.ShapeDtypeStruct((per, share, chunk, wide), F32)] * targets,
        compiler_params=params(1),
        cost_estimate=pl.CostEstimate(
            flops=6 * chunk * per * slabs * kl * (rows * LANES + ranks) * wide,
            bytes_accessed=8 * chunk * per * slabs * kl * rows * LANES,
            transcendentals=0,
        ),
        name="modes_two_three",
    )(*pieces, weights_two, weights_three, *after)


def held(values, after):
    count = len(values)

    def kernel(*refs):
        for source, target in zip(refs[:count], refs[count + len(after):]):
            target[...] = source[...]

    return pl.pallas_call(
        kernel,
        in_specs=[pl.BlockSpec(memory_space=pltpu.VMEM)] * count + [pl.BlockSpec(memory_space=pl.ANY)] * len(after),
        out_specs=[pl.BlockSpec(memory_space=pltpu.VMEM)] * count,
        out_shape=[jax.ShapeDtypeStruct(v.shape, v.dtype) for v in values],
        compiler_params=pltpu.CompilerParams(vmem_limit_bytes=60 * 2 ** 20),
        name="held",
    )(*values, *after)


def gram_times(pieces, factor, fib, spots):
    per, share, _, wide = pieces[0].shape
    count = len(pieces)
    total = sum(piece.shape[2] for piece in pieces)
    block = min(share, 4)

    def kernel(fib_ref, *refs):
        ins, f_ref, out_ref, acc_ref = refs[:count], refs[count], refs[count + 1], refs[count + 2]
        step = pl.program_id(0)

        @pl.when(step == 0)
        def _():
            acc_ref[...] = jnp.zeros_like(acc_ref)

        found = None
        for g in range(per):
            for p in range(block):
                high, low = split(jnp.concatenate([ref[g, p] for ref in ins], axis=0))
                term = dot(high, jnp.concatenate([high, low], axis=0), NT)
                found = term if found is None else found + term
        acc_ref[...] += found

        @pl.when(step == pl.num_programs(0) - 1)
        def _():
            mixed = acc_ref[:, total:]
            gram = acc_ref[:, :total] + mixed + mixed.T
            target = lax.dot_general(gram, f_ref[...], NN, precision=HIGHEST, preferred_element_type=F32)
            for n, (group, spot) in enumerate(spots):
                at = pl.multiple_of((fib_ref[0] ^ group) * (total // fibs), TILE)
                out_ref[pl.ds(at + spot, TILE), :] = target[n * TILE:(n + 1) * TILE]

    fibs = 1 + max(group for group, _ in spots)
    return pl.pallas_call(
        kernel,
        grid_spec=pltpu.PrefetchScalarGridSpec(
            num_scalar_prefetch=1,
            grid=(share // block,),
            in_specs=[
                pl.BlockSpec((per, block, piece.shape[2], wide), lambda s, fib: (0, s, 0, 0)) for piece in pieces]
            + [pl.BlockSpec(factor.shape, lambda s, fib: (0, 0))],
            out_specs=pl.BlockSpec(factor.shape, lambda s, fib: (0, 0)),
            scratch_shapes=[pltpu.VMEM((total, 2 * total), F32)],
        ),
        out_shape=jax.ShapeDtypeStruct(factor.shape, F32),
        compiler_params=params(1),
        name="gram",
    )(fib, *pieces, factor)


def core_parts(pieces, updated, me, first, pairs, parts):
    per, _, _, wide = pieces[0].shape
    count = len(pieces)
    ranks = updated.shape[1]
    m = wide // ranks
    width = ranks // parts

    def kernel(me_ref, *refs):
        ins, u_ref, outs, t_ref, w_ref = refs[:count], refs[count], refs[count + 1:-2], refs[-2], refs[-1]

        @pl.when(pl.program_id(0) == 0)
        def _():
            high, low = split(u_ref[...].T)
            w_ref[...] = jnp.concatenate(
                [jnp.concatenate([high, high], 1), jnp.concatenate([low, jnp.zeros_like(low)], 1)], 0)

        for g in range(per):
            pair = []
            for p in range(2):
                high, low = split(jnp.concatenate([ref[g, p] for ref in ins], axis=0))
                found = dot(w_ref[...], jnp.concatenate([high, low], axis=0))
                pair.append(found[:ranks] + found[ranks:])
            t_ref[g] = jnp.concatenate(pair, axis=0).T.reshape(m, parts, width, 2 * ranks)
        for g in range(per):
            for part in range(parts):
                for r in range(m):
                    outs[part][0, g * m + r] = t_ref[g, r, me_ref[0] ^ part]

    shape = (pairs, per * m, width, 2 * ranks)
    return pl.pallas_call(
        kernel,
        grid_spec=pltpu.PrefetchScalarGridSpec(
            num_scalar_prefetch=1,
            grid=(pairs,),
            in_specs=[
                pl.BlockSpec((per, 2, piece.shape[2], wide), lambda s, me: (0, first + s, 0, 0)) for piece in pieces]
            + [pl.BlockSpec(updated.shape, lambda s, me: (0, 0))],
            out_specs=[pl.BlockSpec((1,) + shape[1:], lambda s, me: (s, 0, 0, 0))] * parts,
            scratch_shapes=[
                pltpu.VMEM((per, m, parts, width, 2 * ranks), F32),
                pltpu.VMEM((2 * ranks, 2 * updated.shape[0]), BF16)],
        ),
        out_shape=[jax.ShapeDtypeStruct(shape, F32)] * parts,
        compiler_params=params(1),
        name="core",
    )(me, *pieces, updated)


def assemble(parts, me, ranks, number, total, whole):
    pairs, own, width, lanes = parts[0].shape
    count = len(parts)

    def kernel(me_ref, *refs):
        ins, out_ref, s_ref = refs[:count], refs[-2], refs[-1]
        for pair in range(pairs):
            for part in range(count):
                s_ref[pair, pl.ds((me_ref[0] ^ part) * own, own)] = ins[part][pair]
            for q in range(width):
                turned = s_ref[pair, :, q, :].T
                for p in range(2):
                    out_ref[:, q, 2 * pair + p, :] = turned[p * ranks:(p + 1) * ranks]

    return pl.pallas_call(
        kernel,
        grid_spec=pltpu.PrefetchScalarGridSpec(
            num_scalar_prefetch=1,
            grid=(1,),
            in_specs=[pl.BlockSpec((pairs, own, width, lanes), lambda s, me: (0, 0, 0, 0))] * count
            + [pl.BlockSpec(memory_space=pl.ANY)] * len(whole),
            out_specs=pl.BlockSpec((ranks, width, 2 * pairs, count * own), lambda s, me: (0, 0, number, 0)),
            scratch_shapes=[pltpu.VMEM((pairs, count * own, width, lanes), F32)],
        ),
        out_shape=jax.ShapeDtypeStruct((ranks, width, 2 * pairs * total, count * own), F32),
        input_output_aliases={1 + count: 0} if whole else {},
        compiler_params=params(1, 16),
        name="assemble",
    )(me, *parts, *whole)


def orthonormal(target, fib, spots):
    total, ranks = target.shape
    tile = 8

    fibs = 1 + max(group for group, _ in spots)

    def kernel(fib_ref, t_ref, out_ref, order_ref):
        z = t_ref[...]
        row = lax.broadcasted_iota(jnp.int32, (tile, 2 * ranks), 0)
        across = lax.broadcasted_iota(jnp.int32, (ranks, ranks), 1)
        down = lax.broadcasted_iota(jnp.int32, (ranks, ranks), 0)
        eye = jnp.where(across == down, jnp.float32(1), jnp.float32(0))
        for repeat in range(2):
            crossed = lax.dot_general(
                z, z, (((0,), (0,)), ((), ())), precision=HIGHEST, preferred_element_type=F32)
            whole = jnp.concatenate([crossed, eye], axis=1)
            blocks = [whole[b * tile:(b + 1) * tile] for b in range(ranks // tile)]
            for k in range(0, ranks, 2):
                home, spot = divmod(k, tile)
                first = {b: jnp.broadcast_to(blocks[b][:, k:k + 1], (tile, 2 * ranks))
                         for b in range(home, len(blocks))}
                second = {b: jnp.broadcast_to(blocks[b][:, k + 1:k + 2], (tile, 2 * ranks))
                          for b in range(home, len(blocks))}
                scale_one = lax.rsqrt(first[home][spot:spot + 1])
                side = first[home][spot + 1:spot + 2] * scale_one
                scale_two = lax.rsqrt(second[home][spot + 1:spot + 2] - side * side)
                one = blocks[home][spot:spot + 1] * scale_one
                two = (blocks[home][spot + 1:spot + 2] - side * one) * scale_two
                for b in range(home, len(blocks)):
                    left = first[b] * scale_one
                    right = (second[b] - side * left) * scale_two
                    fresh = blocks[b] - left * one - right * two
                    if b == home:
                        fresh = jnp.where(row > spot + 1, fresh, blocks[b])
                        fresh = jnp.where(row == spot, one, jnp.where(row == spot + 1, two, fresh))
                    blocks[b] = fresh
            inverse = jnp.concatenate(blocks, axis=0)[:, ranks:]
            z = lax.dot_general(z, inverse, NT, precision=HIGHEST, preferred_element_type=F32)
        out_ref[...] = z
        for n, (group, spot) in enumerate(spots):
            at = pl.multiple_of((fib_ref[0] ^ group) * (total // fibs), TILE)
            order_ref[n * TILE:(n + 1) * TILE, :] = out_ref[pl.ds(at + spot, TILE), :]

    return pl.pallas_call(
        kernel,
        in_specs=[pl.BlockSpec(memory_space=pltpu.SMEM), pl.BlockSpec(memory_space=pltpu.VMEM)],
        out_specs=[pl.BlockSpec(memory_space=pltpu.VMEM)] * 2,
        out_shape=[jax.ShapeDtypeStruct(target.shape, F32)] * 2,
        compiler_params=params(0),
        name="orthonormal",
    )(fib, target)


def body(fibs, rows, slabs, tensor, factor_one, factor_two, factor_three, factor_four):
    both = ("row", "slab")
    grid = rows * slabs
    il, jl, _, _ = tensor.shape
    ranks = factor_four.shape[1]
    m = LANES // jl
    sizes = [TILE] * (il // TILE)
    fib = lax.axis_index("fib")
    place = lax.axis_index("row") * slabs + lax.axis_index("slab")
    me = place.reshape(1).astype(jnp.int32)

    tensor = in_hbm(tensor)
    far = list(range(grid // 2, grid))
    near = list(range(slabs, grid // 2)) + list(range(1, slabs))
    order = [b for pair in itertools.zip_longest(far, near) for b in pair if b is not None] + [0]
    sent, pieces = [], []

    def send(after):
        c = len(sent)
        parts = contract_four(tensor, factor_four, me, sum(sizes[:c]), sizes[c], grid, after)
        sent.append([partner(parts[b], both, grid, b) if b else parts[b] for b in order])

    send([])
    if len(sizes) > 1:
        send([sent[0][0]])
    factor_two, factor_three = held([factor_two, factor_three], [sent[0][3]])
    two = spread(gathered(factor_two, "row", rows), m)
    three = jnp.concatenate(gathered(relative(factor_three, 1, fibs, fib), "slab", slabs)).T
    high, low = split_outside(three)
    three = jnp.concatenate([high, high, low], axis=1)

    for c in range(len(sizes)):
        shares = contract_two_three(sent[c], order, two, three, rows, slabs, fibs, pieces[-fibs:])
        pieces.append(shares[0])
        for b in range(1, fibs):
            pieces.append(partner(shares[b], "fib", fibs, b))
        if c + 2 < len(sizes):
            send([shares[0]])

    def local_order(x):
        y = relative(x, 0, fibs, fib).reshape(fibs, il, ranks)
        starts = [sum(sizes[:c]) for c in range(len(sizes))]
        return jnp.concatenate([y[:, at:at + n].reshape(fibs * n, ranks) for at, n in zip(starts, sizes)])

    spots = [(a, sum(sizes[:c])) for c in range(len(sizes)) for a in range(fibs)]
    here = fib.reshape(1).astype(jnp.int32)
    target = gram_times(pieces, local_order(factor_one), here, spots)
    for axis, count in (("slab", slabs), ("row", rows), ("fib", fibs)):
        target = tree_sum(gathered(target, axis, count))
    updated, ordered = orthonormal(target, here, spots)

    pairs = pieces[0].shape[1] // 2
    total = max(1, pairs // 4)
    pairs //= total
    got = []
    for n in range(total):
        parts = core_parts(pieces, ordered, me, n * pairs, pairs, grid)
        got.append([parts[0]] + [partner(parts[b], both, grid, b) for b in range(1, grid)])
    whole = []
    for n in range(total):
        whole = [assemble(got[n], me, ranks, n, total, whole)]
    return (updated, whole[0])


def solution(mesh):
    in_specs = (P("fib", "row", "slab", None), P(), P("row", None), P("slab", None), P())
    out_specs = (P(), P(None, ("row", "slab"), "fib", None))
    sizes = [mesh.shape[axis] for axis in ("fib", "row", "slab")]
    return jax.shard_map(
        functools.partial(body, *sizes), mesh=mesh, in_specs=in_specs, out_specs=out_specs, check_vma=False)
```

```python
import functools
import itertools

import jax
import jax.numpy as jnp
from jax import lax
from jax.experimental import pallas as pl
from jax.experimental.pallas import tpu as pltpu
from jax.sharding import PartitionSpec as P

F32 = jnp.float32
BF16 = jnp.bfloat16
HIGHEST = lax.Precision.HIGHEST
LANES = 128
TILE = 8
NT = (((1,), (1,)), ((), ()))
NN = (((1,), (0,)), ((), ()))


def split(x):
    high = x.astype(BF16)
    return high, (x - high.astype(F32)).astype(BF16)


def split_outside(x):
    high = lax.reduce_precision(x, 8, 7)
    return high.astype(BF16), (x - high).astype(BF16)


def dot(a, b, dims=NN):
    return lax.dot_general(a, b, dims, preferred_element_type=F32)


def relative(x, axis, count, me):
    shape = x.shape
    width = 1
    while width < count:
        cut = shape[:axis] + (count // (2 * width), 2, shape[axis] // count * width) + shape[axis + 1:]
        y = x.reshape(cut)
        x = jnp.where((me // width) % 2 == 1, jnp.flip(y, axis + 1), y).reshape(shape)
        width *= 2
    return x


def partner(x, axes, count, distance):
    return lax.ppermute(x, axes, [(s, s ^ distance) for s in range(count)])


def in_hbm(x):
    return pltpu.with_memory_space_constraint(x, pltpu.HBM)


def gathered(x, axes, count):
    return [x] + [partner(x, axes, count, b) for b in range(1, count)]


def params(steps, megabytes=12):
    return pltpu.CompilerParams(
        dimension_semantics=("arbitrary",) * steps, vmem_limit_bytes=megabytes * 2 ** 20
    )


def contract_four(tensor, factor, me, first, chunk, parts, after, riders, carriers):
    _, jl, kl, depth = tensor.shape
    ranks = factor.shape[1]
    m = LANES // jl
    groups = kl // m
    own = ranks // parts
    per = own // m
    steps = chunk + 1 if riders else chunk

    def kernel(me_ref, x_ref, f_ref, *refs):
        outs, w_ref, s_ref = refs[len(after) + len(riders):-2], refs[-2], refs[-1]
        step = pl.program_id(0)

        @pl.when(step == 0)
        def _():
            high, low = split(f_ref[...].T)
            w_ref[...] = jnp.concatenate(
                [jnp.concatenate([high, high], 1), jnp.concatenate([low, jnp.zeros_like(low)], 1)], 0)

        if riders:
            @pl.when(step == chunk)
            def _():
                loads = jnp.concatenate([ref[...] for ref in refs[:len(riders)]], axis=1)
                for part in carriers:
                    outs[part][0] = jnp.zeros((per, kl, LANES), F32)
                    outs[part][0, 0] = loads

            @pl.when(step < chunk)
            def _():
                work(me_ref, x_ref, outs, w_ref, s_ref)
        else:
            work(me_ref, x_ref, outs, w_ref, s_ref)

    def work(me_ref, x_ref, outs, w_ref, s_ref):
        lane = lax.broadcasted_iota(jnp.int32, (1, 1, LANES), 2)
        weights = w_ref[...]
        for group in range(groups):
            rows = jnp.concatenate([x_ref[0, :, q * groups + group, :] for q in range(m)], axis=0)
            high, low = split(rows)
            found = dot(weights, jnp.concatenate([high, low], axis=1), NT)
            s_ref[:, group, :] = found[:ranks] + found[ranks:]
        for part in range(parts):
            mine = s_ref[pl.ds((me_ref[0] ^ part) * own, own)].reshape(per, m, groups, LANES)
            blocks = [mine[:, q] for q in range(m)]
            width = m // 2
            while width:
                upper = (lane // (jl * width)) % 2 == 1
                shift = jl * width
                for q in range(m):
                    if q & width == 0:
                        a, b = blocks[q], blocks[q + width]
                        blocks[q] = jnp.where(upper, pltpu.roll(b, shift, 2), a)
                        blocks[q + width] = jnp.where(upper, b, pltpu.roll(a, LANES - shift, 2))
                width //= 2
            for q in range(m):
                outs[part][0, :, q * groups:(q + 1) * groups, :] = blocks[q]

    return pl.pallas_call(
        kernel,
        grid_spec=pltpu.PrefetchScalarGridSpec(
            num_scalar_prefetch=1,
            grid=(steps,),
            in_specs=[
                pl.BlockSpec((1, jl, kl, depth), lambda i, me: (first + jnp.minimum(i, chunk - 1), 0, 0, 0)),
                pl.BlockSpec(factor.shape, lambda i, me: (0, 0)),
            ] + [pl.BlockSpec(rider.shape, lambda i, me: (0, 0)) for rider in riders]
            + [pl.BlockSpec(memory_space=pl.ANY)] * len(after),
            out_specs=[
                pl.BlockSpec((1, per, kl, LANES), lambda i, me: (i, 0, 0, 0)) if riders and part in carriers else
                pl.BlockSpec((1, per, kl, LANES), lambda i, me: (jnp.minimum(i, chunk - 1), 0, 0, 0))
                for part in range(parts)],
            scratch_shapes=[
                pltpu.VMEM((2 * ranks, 2 * depth), BF16), pltpu.VMEM((ranks, groups, LANES), F32)],
        ),
        out_shape=[
            jax.ShapeDtypeStruct((steps if part in carriers else chunk, per, kl, LANES), F32)
            for part in range(parts)],
        compiler_params=params(1),
        cost_estimate=pl.CostEstimate(
            flops=12 * chunk * jl * kl * depth * ranks, bytes_accessed=6 * chunk * jl * kl * depth, transcendentals=0
        ),
        name="mode_four",
    )(me, tensor, factor, *riders, *after)


def spread(own, carried, m, after):
    jl, ranks = own.shape
    count = 1 + len(carried)
    rows, wide = count * m * jl, m * ranks

    def kernel(*refs):
        out_ref = refs[-1]
        out_ref[...] = jnp.zeros_like(out_ref)
        for n, ref in enumerate(refs[:count]):
            for half, value in enumerate(split(ref[0, 0, :, :ranks] if n else ref[...])):
                for r in range(m):
                    at = (n * m + r) * jl
                    out_ref[at:at + jl, half * wide + r * ranks:half * wide + (r + 1) * ranks] = value

    return pl.pallas_call(
        kernel,
        grid=(1,),
        in_specs=[pl.BlockSpec((jl, ranks), lambda s: (0, 0))]
        + [pl.BlockSpec((1, 1, jl, LANES), lambda s, last=x.shape[0] - 1: (last, 0, 0, 0)) for x in carried]
        + [pl.BlockSpec(memory_space=pl.ANY)] * len(after),
        out_specs=pl.BlockSpec((rows, 2 * wide), lambda s: (0, 0)),
        out_shape=jax.ShapeDtypeStruct((rows, 2 * wide), BF16),
        compiler_params=params(1),
        name="spread",
    )(own, *carried, *after)


def contract_two_three(pieces, order, weights_two, weights_three, rows, slabs, targets, after):
    chunk, per, kl, _ = pieces[-1].shape
    wide = weights_two.shape[1] // 2
    ranks = weights_three.shape[0]
    share = ranks // targets
    count = len(pieces)

    def kernel(*refs):
        ins, two_ref, three_ref, outs = refs[:count], refs[count], refs[count + 1], refs[count + 2 + len(after):]
        taken = []
        for slab in range(slabs):
            taken.append(jnp.concatenate(
                [ins[order.index(row * slabs + slab)][...].reshape(chunk * kl, LANES) for row in range(rows)], axis=1))
        high, low = split(jnp.concatenate(taken, axis=0))
        two_high, two_low = two_ref[:, :wide], two_ref[:, wide:]
        half = dot(high, two_high) + dot(low, two_high) + dot(high, two_low)
        high, low = split(half)
        for i in range(chunk):
            spots = [slice((slab * chunk + i) * kl, (slab * chunk + i + 1) * kl) for slab in range(slabs)]
            own_high = jnp.concatenate([high[s] for s in spots], axis=0)
            own_low = jnp.concatenate([low[s] for s in spots], axis=0)
            full = dot(three_ref[...], jnp.concatenate([own_high, own_low, own_high], axis=0))
            for target in range(targets):
                outs[target][0, :, i, :] = full[target * share:(target + 1) * share]

    return pl.pallas_call(
        kernel,
        grid=(per,),
        in_specs=[pl.BlockSpec((chunk, 1, kl, LANES), lambda g: (0, g, 0, 0))] * count
        + [
            pl.BlockSpec(weights_two.shape, lambda g: (0, 0)),
            pl.BlockSpec(weights_three.shape, lambda g: (0, 0)),
        ] + [pl.BlockSpec(memory_space=pl.ANY)] * len(after),
        out_specs=[pl.BlockSpec((1, share, chunk, wide), lambda g: (g, 0, 0, 0))] * targets,
        out_shape=[jax.ShapeDtypeStruct((per, share, chunk, wide), F32)] * targets,
        compiler_params=params(1),
        cost_estimate=pl.CostEstimate(
            flops=6 * chunk * per * slabs * kl * (rows * LANES + ranks) * wide,
            bytes_accessed=8 * chunk * per * slabs * kl * rows * LANES,
            transcendentals=0,
        ),
        name="modes_two_three",
    )(*pieces, weights_two, weights_three, *after)


def gram_times(pieces, factor, fib, spots):
    per, share, _, wide = pieces[0].shape
    count = len(pieces)
    total = sum(piece.shape[2] for piece in pieces)
    block = min(share, 4)

    def kernel(fib_ref, *refs):
        ins, f_ref, out_ref, acc_ref = refs[:count], refs[count], refs[count + 1], refs[count + 2]
        step = pl.program_id(0)

        @pl.when(step == 0)
        def _():
            acc_ref[...] = jnp.zeros_like(acc_ref)

        found = None
        for g in range(per):
            for p in range(block):
                high, low = split(jnp.concatenate([ref[g, p] for ref in ins], axis=0))
                term = dot(high, jnp.concatenate([high, low], axis=0), NT)
                found = term if found is None else found + term
        acc_ref[...] += found

        @pl.when(step == pl.num_programs(0) - 1)
        def _():
            mixed = acc_ref[:, total:]
            gram = acc_ref[:, :total] + mixed + mixed.T
            target = lax.dot_general(gram, f_ref[...], NN, precision=HIGHEST, preferred_element_type=F32)
            for n, (group, spot) in enumerate(spots):
                at = pl.multiple_of((fib_ref[0] ^ group) * (total // fibs), TILE)
                out_ref[pl.ds(at + spot, TILE), :] = target[n * TILE:(n + 1) * TILE]

    fibs = 1 + max(group for group, _ in spots)
    return pl.pallas_call(
        kernel,
        grid_spec=pltpu.PrefetchScalarGridSpec(
            num_scalar_prefetch=1,
            grid=(share // block,),
            in_specs=[
                pl.BlockSpec((per, block, piece.shape[2], wide), lambda s, fib: (0, s, 0, 0)) for piece in pieces]
            + [pl.BlockSpec(factor.shape, lambda s, fib: (0, 0))],
            out_specs=pl.BlockSpec(factor.shape, lambda s, fib: (0, 0)),
            scratch_shapes=[pltpu.VMEM((total, 2 * total), F32)],
        ),
        out_shape=jax.ShapeDtypeStruct(factor.shape, F32),
        compiler_params=params(1),
        name="gram",
    )(fib, *pieces, factor)


def core_parts(pieces, updated, me, first, pairs, parts):
    per, _, _, wide = pieces[0].shape
    count = len(pieces)
    ranks = updated.shape[1]
    m = wide // ranks
    width = ranks // parts

    def kernel(me_ref, *refs):
        ins, u_ref, outs, t_ref, w_ref = refs[:count], refs[count], refs[count + 1:-2], refs[-2], refs[-1]

        @pl.when(pl.program_id(0) == 0)
        def _():
            high, low = split(u_ref[...].T)
            w_ref[...] = jnp.concatenate(
                [jnp.concatenate([high, high], 1), jnp.concatenate([low, jnp.zeros_like(low)], 1)], 0)

        for g in range(per):
            pair = []
            for p in range(2):
                high, low = split(jnp.concatenate([ref[g, p] for ref in ins], axis=0))
                found = dot(w_ref[...], jnp.concatenate([high, low], axis=0))
                pair.append(found[:ranks] + found[ranks:])
            t_ref[g] = jnp.concatenate(pair, axis=0).T.reshape(m, parts, width, 2 * ranks)
        for g in range(per):
            for part in range(parts):
                for r in range(m):
                    outs[part][0, g * m + r] = t_ref[g, r, me_ref[0] ^ part]

    shape = (pairs, per * m, width, 2 * ranks)
    return pl.pallas_call(
        kernel,
        grid_spec=pltpu.PrefetchScalarGridSpec(
            num_scalar_prefetch=1,
            grid=(pairs,),
            in_specs=[
                pl.BlockSpec((per, 2, piece.shape[2], wide), lambda s, me: (0, first + s, 0, 0)) for piece in pieces]
            + [pl.BlockSpec(updated.shape, lambda s, me: (0, 0))],
            out_specs=[pl.BlockSpec((1,) + shape[1:], lambda s, me: (s, 0, 0, 0))] * parts,
            scratch_shapes=[
                pltpu.VMEM((per, m, parts, width, 2 * ranks), F32),
                pltpu.VMEM((2 * ranks, 2 * updated.shape[0]), BF16)],
        ),
        out_shape=[jax.ShapeDtypeStruct(shape, F32)] * parts,
        compiler_params=params(1),
        name="core",
    )(me, *pieces, updated)


def assemble(parts, order, me, ranks, number, total, whole):
    pairs, own, width, lanes = parts[0].shape
    count = len(parts)

    def kernel(me_ref, *refs):
        ins, out_ref, s_ref = refs[:count], refs[-2], refs[-1]
        for pair in range(pairs):
            for ref, part in zip(ins, order):
                s_ref[pair, pl.ds((me_ref[0] ^ part) * own, own)] = ref[pair]
            for q in range(width):
                turned = s_ref[pair, :, q, :].T
                for p in range(2):
                    out_ref[:, q, 2 * pair + p, :] = turned[p * ranks:(p + 1) * ranks]

    return pl.pallas_call(
        kernel,
        grid_spec=pltpu.PrefetchScalarGridSpec(
            num_scalar_prefetch=1,
            grid=(1,),
            in_specs=[pl.BlockSpec((pairs, own, width, lanes), lambda s, me: (0, 0, 0, 0))] * count
            + [pl.BlockSpec(memory_space=pl.ANY)] * len(whole),
            out_specs=pl.BlockSpec((ranks, width, 2 * pairs, count * own), lambda s, me: (0, 0, number, 0)),
            scratch_shapes=[pltpu.VMEM((pairs, count * own, width, lanes), F32)],
        ),
        out_shape=jax.ShapeDtypeStruct((ranks, width, 2 * pairs * total, count * own), F32),
        input_output_aliases={1 + count: 0} if whole else {},
        compiler_params=params(1, 16),
        name="assemble",
    )(me, *parts, *whole)


def orthonormal(target, fib, spots):
    total, ranks = target.shape
    tile = 8

    fibs = 1 + max(group for group, _ in spots)

    def kernel(fib_ref, t_ref, out_ref, order_ref):
        z = t_ref[...]
        row = lax.broadcasted_iota(jnp.int32, (tile, 2 * ranks), 0)
        across = lax.broadcasted_iota(jnp.int32, (ranks, ranks), 1)
        down = lax.broadcasted_iota(jnp.int32, (ranks, ranks), 0)
        eye = jnp.where(across == down, jnp.float32(1), jnp.float32(0))
        for repeat in range(2):
            crossed = lax.dot_general(
                z, z, (((0,), (0,)), ((), ())), precision=HIGHEST, preferred_element_type=F32)
            whole = jnp.concatenate([crossed, eye], axis=1)
            blocks = [whole[b * tile:(b + 1) * tile] for b in range(ranks // tile)]
            for k in range(0, ranks, 2):
                home, spot = divmod(k, tile)
                first = {b: jnp.broadcast_to(blocks[b][:, k:k + 1], (tile, 2 * ranks))
                         for b in range(home, len(blocks))}
                second = {b: jnp.broadcast_to(blocks[b][:, k + 1:k + 2], (tile, 2 * ranks))
                          for b in range(home, len(blocks))}
                scale_one = lax.rsqrt(first[home][spot:spot + 1])
                side = first[home][spot + 1:spot + 2] * scale_one
                scale_two = lax.rsqrt(second[home][spot + 1:spot + 2] - side * side)
                one = blocks[home][spot:spot + 1] * scale_one
                two = (blocks[home][spot + 1:spot + 2] - side * one) * scale_two
                for b in range(home, len(blocks)):
                    left = first[b] * scale_one
                    right = (second[b] - side * left) * scale_two
                    fresh = blocks[b] - left * one - right * two
                    if b == home:
                        fresh = jnp.where(row > spot + 1, fresh, blocks[b])
                        fresh = jnp.where(row == spot, one, jnp.where(row == spot + 1, two, fresh))
                    blocks[b] = fresh
            inverse = jnp.concatenate(blocks, axis=0)[:, ranks:]
            z = lax.dot_general(z, inverse, NT, precision=HIGHEST, preferred_element_type=F32)
        out_ref[...] = z
        for n, (group, spot) in enumerate(spots):
            at = pl.multiple_of((fib_ref[0] ^ group) * (total // fibs), TILE)
            order_ref[n * TILE:(n + 1) * TILE, :] = out_ref[pl.ds(at + spot, TILE), :]

    return pl.pallas_call(
        kernel,
        in_specs=[pl.BlockSpec(memory_space=pltpu.SMEM), pl.BlockSpec(memory_space=pltpu.VMEM)],
        out_specs=[pl.BlockSpec(memory_space=pltpu.VMEM)] * 2,
        out_shape=[jax.ShapeDtypeStruct(target.shape, F32)] * 2,
        compiler_params=params(0),
        name="orthonormal",
    )(fib, target)


def body(fibs, rows, slabs, tensor, factor_one, factor_two, factor_three, factor_four):
    both = ("row", "slab")
    grid = rows * slabs
    il, jl, _, _ = tensor.shape
    ranks = factor_four.shape[1]
    m = LANES // jl
    sizes = [TILE] * (il // TILE)
    fib = lax.axis_index("fib")
    place = lax.axis_index("row") * slabs + lax.axis_index("slab")
    me = place.reshape(1).astype(jnp.int32)

    tensor = in_hbm(tensor)
    far = list(range(grid // 2, grid))
    near = list(range(slabs, grid // 2)) + list(range(1, slabs))
    order = [b for pair in itertools.zip_longest(far, near) for b in pair if b is not None] + [0]
    sent, pieces = [], []

    carriers = [b for b in range(1, grid) if b < slabs or b % slabs == 0]

    def send(after, riders=()):
        c = len(sent)
        parts = contract_four(
            tensor, factor_four, me, sum(sizes[:c]), sizes[c], grid, after, riders, carriers if riders else ())
        sent.append([partner(parts[b], both, grid, b) if b else parts[b] for b in order])

    send([], [factor_two, factor_three])
    if len(sizes) > 1:
        send([sent[0][0]])
    two = spread(factor_two, [sent[0][order.index(b)] for b in range(slabs, grid, slabs)], m, [sent[-1][-1]])
    three = [factor_three] + [sent[0][order.index(b)][-1, 0, :, ranks:] for b in range(1, slabs)]
    three = relative(jnp.concatenate(three), 1, fibs, fib).T
    high, low = split_outside(three)
    three = jnp.concatenate([high, high, low], axis=1)

    for c in range(len(sizes)):
        after = pieces[max(0, c - 1) * fibs:] if c < len(sizes) - 1 else pieces[max(0, c - 2) * fibs:(c - 1) * fibs]
        if c + 2 < len(sizes):
            send([sent[max(c, 1)][0]])
            after = after + [sent[-1][-1]]
        shares = contract_two_three(sent[c], order, two, three, rows, slabs, fibs, after)
        pieces.append(shares[0])
        for b in range(1, fibs):
            pieces.append(partner(shares[b], "fib", fibs, b))

    def local_order(x):
        y = relative(x, 0, fibs, fib).reshape(fibs, il, ranks)
        starts = [sum(sizes[:c]) for c in range(len(sizes))]
        return jnp.concatenate([y[:, at:at + n].reshape(fibs * n, ranks) for at, n in zip(starts, sizes)])

    spots = [(a, sum(sizes[:c])) for c in range(len(sizes)) for a in range(fibs)]
    here = fib.reshape(1).astype(jnp.int32)
    target = gram_times(pieces, local_order(factor_one), here, spots)
    for axis, count in (("slab", slabs), ("row", rows), ("fib", fibs)):
        distance = 1
        while distance < count:
            target = target + partner(target, axis, count, distance)
            distance *= 2
    updated, ordered = orthonormal(target, here, spots)

    pairs = pieces[0].shape[1] // 2
    total = max(1, pairs // 4)
    pairs //= total
    got = []
    for n in range(total):
        parts = core_parts(pieces, ordered, me, n * pairs, pairs, grid)
        got.append([partner(parts[b], both, grid, b) if b else parts[b] for b in order])
    whole = []
    for n in range(total):
        whole = [assemble(got[n], order, me, ranks, n, total, whole)]
    return (updated, whole[0])


def solution(mesh):
    in_specs = (P("fib", "row", "slab", None), P(), P("row", None), P("slab", None), P())
    out_specs = (P(), P(None, ("row", "slab"), "fib", None))
    sizes = [mesh.shape[axis] for axis in ("fib", "row", "slab")]
    return jax.shard_map(
        functools.partial(body, *sizes), mesh=mesh, in_specs=in_specs, out_specs=out_specs, check_vma=False)
```

```python
import functools
import itertools

import jax
import jax.numpy as jnp
from jax import lax
from jax.experimental import pallas as pl
from jax.experimental.pallas import tpu as pltpu
from jax.sharding import PartitionSpec as P

F32 = jnp.float32
BF16 = jnp.bfloat16
HIGHEST = lax.Precision.HIGHEST
LANES = 128
TILE = 8
PIVOTS = 4
NT = (((1,), (1,)), ((), ()))
NN = (((1,), (0,)), ((), ()))


def split(x):
    high = x.astype(BF16)
    return high, (x - high.astype(F32)).astype(BF16)


def split_outside(x):
    high = lax.reduce_precision(x, 8, 7)
    return high.astype(BF16), (x - high).astype(BF16)


def dot(a, b, dims=NN):
    return lax.dot_general(a, b, dims, preferred_element_type=F32)


def relative(x, axis, count, me):
    shape = x.shape
    width = 1
    while width < count:
        cut = shape[:axis] + (count // (2 * width), 2, shape[axis] // count * width) + shape[axis + 1:]
        y = x.reshape(cut)
        x = jnp.where((me // width) % 2 == 1, jnp.flip(y, axis + 1), y).reshape(shape)
        width *= 2
    return x


def partner(x, axes, count, distance):
    return lax.ppermute(x, axes, [(s, s ^ distance) for s in range(count)])


def in_hbm(x):
    return pltpu.with_memory_space_constraint(x, pltpu.HBM)


def gathered(x, axes, count):
    return [x] + [partner(x, axes, count, b) for b in range(1, count)]


def params(steps, megabytes=12):
    return pltpu.CompilerParams(
        dimension_semantics=("arbitrary",) * steps, vmem_limit_bytes=megabytes * 2 ** 20
    )


def contract_four(tensor, factor, me, first, chunk, parts, after, riders, carriers):
    _, jl, kl, depth = tensor.shape
    ranks = factor.shape[0]
    m = LANES // jl
    groups = kl // m
    cuts = 4
    own = ranks // parts
    per = own // m
    steps = chunk + 1 if riders else chunk

    def kernel(me_ref, *refs):
        x_refs, f_ref, refs = refs[:cuts], refs[cuts], refs[cuts + 1:]
        outs, w_ref, s_ref = refs[len(after) + len(riders):-2], refs[-2], refs[-1]
        step = pl.program_id(0)

        @pl.when(step == 0)
        def _():
            high, low = split(f_ref[...].T)
            none = jnp.zeros_like(high)
            left, right = [jnp.concatenate(pair, axis=1) for pair in ((high, none), (none, high))]
            w_ref[...] = jnp.concatenate(
                [left, left, right, right, jnp.concatenate([low, none], 1), jnp.concatenate([none, low], 1)], 0)

        if riders:
            @pl.when(step == chunk)
            def _():
                loads = jnp.concatenate([ref[...] for ref in refs[:len(riders)]], axis=1)
                for part in carriers:
                    outs[part][0] = jnp.zeros((per, kl, LANES), F32)
                    outs[part][0, 0] = loads

            @pl.when(step < chunk)
            def _():
                work(me_ref, x_refs, outs, w_ref, s_ref)
        else:
            work(me_ref, x_refs, outs, w_ref, s_ref)

    def work(me_ref, x_refs, outs, w_ref, s_ref):
        lane = lax.broadcasted_iota(jnp.int32, (1, 1, LANES), 2)
        half = groups // 2
        found = []
        for side in range(2):
            rows = jnp.concatenate([
                x_ref[0, :, q * groups + side * half + n, :]
                for n in range(half) for q in range(m) for x_ref in x_refs], axis=0)
            found += split(rows)
        found = dot(jnp.concatenate(found, axis=1), w_ref[:4 * depth]) + dot(
            jnp.concatenate(found[::2], axis=1), w_ref[4 * depth:])
        for n in range(half):
            turned = found[n * LANES:(n + 1) * LANES].T
            s_ref[:, n, :] = turned[:ranks]
            s_ref[:, half + n, :] = turned[ranks:]
        for part in range(parts):
            mine = s_ref[pl.ds((me_ref[0] ^ part) * own, own)].reshape(per, m, groups, LANES)
            blocks = [mine[:, q] for q in range(m)]
            width = m // 2
            while width:
                upper = (lane // (jl * width)) % 2 == 1
                shift = jl * width
                for q in range(m):
                    if q & width == 0:
                        a, b = blocks[q], blocks[q + width]
                        blocks[q] = jnp.where(upper, pltpu.roll(b, shift, 2), a)
                        blocks[q + width] = jnp.where(upper, b, pltpu.roll(a, LANES - shift, 2))
                width //= 2
            for q in range(m):
                outs[part][0, :, q * groups:(q + 1) * groups, :] = blocks[q]

    return pl.pallas_call(
        kernel,
        grid_spec=pltpu.PrefetchScalarGridSpec(
            num_scalar_prefetch=1,
            grid=(steps,),
            in_specs=[
                pl.BlockSpec(
                    (1, jl // cuts, kl, depth),
                    lambda i, me, cut=cut: (first + jnp.minimum(i, chunk - 1), cut, 0, 0)) for cut in range(cuts)
            ] + [
                pl.BlockSpec(factor.shape, lambda i, me: (0, 0)),
            ] + [pl.BlockSpec(rider.shape, lambda i, me: (0, 0)) for rider in riders]
            + [pl.BlockSpec(memory_space=pl.ANY)] * len(after),
            out_specs=[
                pl.BlockSpec((1, per, kl, LANES), lambda i, me: (i, 0, 0, 0)) if riders and part in carriers else
                pl.BlockSpec((1, per, kl, LANES), lambda i, me: (jnp.minimum(i, chunk - 1), 0, 0, 0))
                for part in range(parts)],
            scratch_shapes=[
                pltpu.VMEM((6 * depth, 2 * ranks), BF16), pltpu.VMEM((ranks, groups, LANES), F32)],
        ),
        out_shape=[
            jax.ShapeDtypeStruct((steps if part in carriers else chunk, per, kl, LANES), F32)
            for part in range(parts)],
        compiler_params=params(1),
        cost_estimate=pl.CostEstimate(
            flops=12 * chunk * jl * kl * depth * ranks, bytes_accessed=6 * chunk * jl * kl * depth, transcendentals=0
        ),
        name="mode_four",
    )(me, *[tensor] * cuts, factor, *riders, *after)


def spread(own, carried, m, after):
    jl, ranks = own.shape
    count = 1 + len(carried)
    rows, wide = count * m * jl, m * ranks

    def kernel(*refs):
        out_ref = refs[-1]
        out_ref[...] = jnp.zeros_like(out_ref)
        for n, ref in enumerate(refs[:count]):
            for half, value in enumerate(split(ref[0, 0, :, :ranks] if n else ref[...])):
                for r in range(m):
                    at = (n * m + r) * jl
                    out_ref[at:at + jl, half * wide + r * ranks:half * wide + (r + 1) * ranks] = value

    return pl.pallas_call(
        kernel,
        grid=(1,),
        in_specs=[pl.BlockSpec((jl, ranks), lambda s: (0, 0))]
        + [pl.BlockSpec((1, 1, jl, LANES), lambda s, last=x.shape[0] - 1: (last, 0, 0, 0)) for x in carried]
        + [pl.BlockSpec(memory_space=pl.ANY)] * len(after),
        out_specs=pl.BlockSpec((rows, 2 * wide), lambda s: (0, 0)),
        out_shape=jax.ShapeDtypeStruct((rows, 2 * wide), BF16),
        compiler_params=params(1),
        name="spread",
    )(own, *carried, *after)


def contract_two_three(pieces, order, weights_two, weights_three, rows, slabs, targets, after):
    chunk, per, kl, _ = pieces[-1].shape
    wide = weights_two.shape[1] // 2
    ranks = weights_three.shape[0]
    share = ranks // targets
    count = len(pieces)

    def kernel(*refs):
        ins, two_ref, three_ref, outs = refs[:count], refs[count], refs[count + 1], refs[count + 2 + len(after):]
        taken = []
        for slab in range(slabs):
            taken.append(jnp.concatenate(
                [ins[order.index(row * slabs + slab)][...].reshape(chunk * kl, LANES) for row in range(rows)], axis=1))
        high, low = split(jnp.concatenate(taken, axis=0))
        two_high, two_low = two_ref[:, :wide], two_ref[:, wide:]
        half = dot(high, two_high) + dot(low, two_high) + dot(high, two_low)
        high, low = split(half)
        for i in range(chunk):
            spots = [slice((slab * chunk + i) * kl, (slab * chunk + i + 1) * kl) for slab in range(slabs)]
            own_high = jnp.concatenate([high[s] for s in spots], axis=0)
            own_low = jnp.concatenate([low[s] for s in spots], axis=0)
            full = dot(three_ref[...], jnp.concatenate([own_high, own_low, own_high], axis=0))
            for target in range(targets):
                outs[target][0, :, i, :] = full[target * share:(target + 1) * share]

    return pl.pallas_call(
        kernel,
        grid=(per,),
        in_specs=[pl.BlockSpec((chunk, 1, kl, LANES), lambda g: (0, g, 0, 0))] * count
        + [
            pl.BlockSpec(weights_two.shape, lambda g: (0, 0)),
            pl.BlockSpec(weights_three.shape, lambda g: (0, 0)),
        ] + [pl.BlockSpec(memory_space=pl.ANY)] * len(after),
        out_specs=[pl.BlockSpec((1, share, chunk, wide), lambda g: (g, 0, 0, 0))] * targets,
        out_shape=[jax.ShapeDtypeStruct((per, share, chunk, wide), F32)] * targets,
        compiler_params=params(1),
        cost_estimate=pl.CostEstimate(
            flops=6 * chunk * per * slabs * kl * (rows * LANES + ranks) * wide,
            bytes_accessed=8 * chunk * per * slabs * kl * rows * LANES,
            transcendentals=0,
        ),
        name="modes_two_three",
    )(*pieces, weights_two, weights_three, *after)


def gram_times(pieces, factor, fib, spots):
    per, share, _, wide = pieces[0].shape
    count = len(pieces)
    total = sum(piece.shape[2] for piece in pieces)
    block = min(share, 4)

    def kernel(fib_ref, *refs):
        ins, f_ref, out_ref, acc_ref = refs[:count], refs[count], refs[count + 1], refs[count + 2]
        step = pl.program_id(0)

        @pl.when(step == 0)
        def _():
            acc_ref[...] = jnp.zeros_like(acc_ref)

        found = None
        for g in range(per):
            for p in range(block):
                high, low = split(jnp.concatenate([ref[g, p] for ref in ins], axis=0))
                term = dot(high, jnp.concatenate([high, low], axis=0), NT)
                found = term if found is None else found + term
        acc_ref[...] += found

        @pl.when(step == pl.num_programs(0) - 1)
        def _():
            mixed = acc_ref[:, total:]
            gram = acc_ref[:, :total] + mixed + mixed.T
            target = lax.dot_general(gram, f_ref[...], NN, precision=HIGHEST, preferred_element_type=F32)
            for n, (group, spot) in enumerate(spots):
                at = pl.multiple_of((fib_ref[0] ^ group) * (total // fibs), TILE)
                out_ref[pl.ds(at + spot, TILE), :] = target[n * TILE:(n + 1) * TILE]

    fibs = 1 + max(group for group, _ in spots)
    return pl.pallas_call(
        kernel,
        grid_spec=pltpu.PrefetchScalarGridSpec(
            num_scalar_prefetch=1,
            grid=(share // block,),
            in_specs=[
                pl.BlockSpec((per, block, piece.shape[2], wide), lambda s, fib: (0, s, 0, 0)) for piece in pieces]
            + [pl.BlockSpec(factor.shape, lambda s, fib: (0, 0))],
            out_specs=pl.BlockSpec(factor.shape, lambda s, fib: (0, 0)),
            scratch_shapes=[pltpu.VMEM((total, 2 * total), F32)],
        ),
        out_shape=jax.ShapeDtypeStruct(factor.shape, F32),
        compiler_params=params(1),
        name="gram",
    )(fib, *pieces, factor)


def core_parts(pieces, updated, me, first, pairs, parts):
    per, _, _, wide = pieces[0].shape
    count = len(pieces)
    ranks = updated.shape[1]
    m = wide // ranks
    width = ranks // parts

    def kernel(me_ref, *refs):
        ins, u_ref, outs, t_ref, w_ref = refs[:count], refs[count], refs[count + 1:-2], refs[-2], refs[-1]

        @pl.when(pl.program_id(0) == 0)
        def _():
            high, low = split(u_ref[...].T)
            w_ref[...] = jnp.concatenate(
                [jnp.concatenate([high, high], 1), jnp.concatenate([low, jnp.zeros_like(low)], 1)], 0)

        for g in range(per):
            pair = []
            for p in range(2):
                high, low = split(jnp.concatenate([ref[g, p] for ref in ins], axis=0))
                found = dot(w_ref[...], jnp.concatenate([high, low], axis=0))
                pair.append(found[:ranks] + found[ranks:])
            t_ref[g] = jnp.concatenate(pair, axis=0).T.reshape(m, parts, width, 2 * ranks)
        for g in range(per):
            for part in range(parts):
                for r in range(m):
                    outs[part][0, g * m + r] = t_ref[g, r, me_ref[0] ^ part]

    shape = (pairs, per * m, width, 2 * ranks)
    return pl.pallas_call(
        kernel,
        grid_spec=pltpu.PrefetchScalarGridSpec(
            num_scalar_prefetch=1,
            grid=(pairs,),
            in_specs=[
                pl.BlockSpec((per, 2, piece.shape[2], wide), lambda s, me: (0, first + s, 0, 0)) for piece in pieces]
            + [pl.BlockSpec(updated.shape, lambda s, me: (0, 0))],
            out_specs=[pl.BlockSpec((1,) + shape[1:], lambda s, me: (s, 0, 0, 0))] * parts,
            scratch_shapes=[
                pltpu.VMEM((per, m, parts, width, 2 * ranks), F32),
                pltpu.VMEM((2 * ranks, 2 * updated.shape[0]), BF16)],
        ),
        out_shape=[jax.ShapeDtypeStruct(shape, F32)] * parts,
        compiler_params=params(1),
        name="core",
    )(me, *pieces, updated)


def assemble(parts, order, me, ranks, number, total, whole):
    pairs, own, width, lanes = parts[0].shape
    count = len(parts)

    def kernel(me_ref, *refs):
        ins, out_ref, s_ref = refs[:count], refs[-2], refs[-1]
        for pair in range(pairs):
            for ref, part in zip(ins, order):
                s_ref[pair, pl.ds((me_ref[0] ^ part) * own, own)] = ref[pair]
            for q in range(width):
                turned = s_ref[pair, :, q, :].T
                for p in range(2):
                    out_ref[:, q, 2 * pair + p, :] = turned[p * ranks:(p + 1) * ranks]

    return pl.pallas_call(
        kernel,
        grid_spec=pltpu.PrefetchScalarGridSpec(
            num_scalar_prefetch=1,
            grid=(1,),
            in_specs=[pl.BlockSpec((pairs, own, width, lanes), lambda s, me: (0, 0, 0, 0))] * count
            + [pl.BlockSpec(memory_space=pl.ANY)] * len(whole),
            out_specs=pl.BlockSpec((ranks, width, 2 * pairs, count * own), lambda s, me: (0, 0, number, 0)),
            scratch_shapes=[pltpu.VMEM((pairs, count * own, width, lanes), F32)],
        ),
        out_shape=jax.ShapeDtypeStruct((ranks, width, 2 * pairs * total, count * own), F32),
        input_output_aliases={1 + count: 0} if whole else {},
        compiler_params=params(1, 16),
        name="assemble",
    )(me, *parts, *whole)


def orthonormal(target, fib, spots):
    total, ranks = target.shape
    tile = 8

    fibs = 1 + max(group for group, _ in spots)

    def kernel(fib_ref, t_ref, out_ref, order_ref):
        z = t_ref[...]
        row = lax.broadcasted_iota(jnp.int32, (tile, 2 * ranks), 0)
        across = lax.broadcasted_iota(jnp.int32, (ranks, ranks), 1)
        down = lax.broadcasted_iota(jnp.int32, (ranks, ranks), 0)
        eye = jnp.where(across == down, jnp.float32(1), jnp.float32(0))
        for repeat in range(2):
            crossed = lax.dot_general(
                z, z, (((0,), (0,)), ((), ())), precision=HIGHEST, preferred_element_type=F32)
            whole = jnp.concatenate([crossed, eye], axis=1)
            blocks = [whole[b * tile:(b + 1) * tile] for b in range(ranks // tile)]
            for k in range(0, ranks, PIVOTS):
                home, spot = divmod(k, tile)
                columns = [
                    {b: jnp.broadcast_to(blocks[b][:, k + t:k + t + 1], (tile, 2 * ranks))
                     for b in range(home, len(blocks))} for t in range(PIVOTS)]
                tops = [blocks[home][spot + t:spot + t + 1] for t in range(PIVOTS)]
                for t in range(PIVOTS):
                    scale = lax.rsqrt(columns[t][home][spot + t:spot + t + 1])
                    tops[t] = tops[t] * scale
                    columns[t] = {b: column * scale for b, column in columns[t].items()}
                    for u in range(t + 1, PIVOTS):
                        side = columns[t][home][spot + u:spot + u + 1]
                        tops[u] = tops[u] - side * tops[t]
                        columns[u] = {b: column - side * columns[t][b] for b, column in columns[u].items()}
                for b in range(home, len(blocks)):
                    fresh = blocks[b]
                    for t in range(PIVOTS):
                        fresh = fresh - columns[t][b] * tops[t]
                    if b == home:
                        fresh = jnp.where(row >= spot + PIVOTS, fresh, blocks[b])
                        for t in range(PIVOTS):
                            fresh = jnp.where(row == spot + t, tops[t], fresh)
                    blocks[b] = fresh
            inverse = jnp.concatenate(blocks, axis=0)[:, ranks:]
            z = lax.dot_general(z, inverse, NT, precision=HIGHEST, preferred_element_type=F32)
        out_ref[...] = z
        for n, (group, spot) in enumerate(spots):
            at = pl.multiple_of((fib_ref[0] ^ group) * (total // fibs), TILE)
            order_ref[n * TILE:(n + 1) * TILE, :] = out_ref[pl.ds(at + spot, TILE), :]

    return pl.pallas_call(
        kernel,
        in_specs=[pl.BlockSpec(memory_space=pltpu.SMEM), pl.BlockSpec(memory_space=pltpu.VMEM)],
        out_specs=[pl.BlockSpec(memory_space=pltpu.VMEM)] * 2,
        out_shape=[jax.ShapeDtypeStruct(target.shape, F32)] * 2,
        compiler_params=params(0),
        name="orthonormal",
    )(fib, target)


def body(fibs, rows, slabs, tensor, factor_one, factor_two, factor_three, factor_four):
    both = ("row", "slab")
    grid = rows * slabs
    il, jl, _, _ = tensor.shape
    ranks = factor_four.shape[1]
    m = LANES // jl
    sizes = [TILE] * (il // TILE)
    fib = lax.axis_index("fib")
    place = lax.axis_index("row") * slabs + lax.axis_index("slab")
    me = place.reshape(1).astype(jnp.int32)

    tensor = in_hbm(tensor)
    far = list(range(grid // 2, grid))
    near = list(range(slabs, grid // 2)) + list(range(1, slabs))
    order = [b for pair in itertools.zip_longest(far, near) for b in pair if b is not None] + [0]
    sent, pieces = [], []

    carriers = [b for b in range(1, grid) if b < slabs or b % slabs == 0]

    def send(after, riders=()):
        c = len(sent)
        parts = contract_four(
            tensor, factor_four.T, me, sum(sizes[:c]), sizes[c], grid, after, riders, carriers if riders else ())
        sent.append([partner(parts[b], both, grid, b) if b else parts[b] for b in order])

    send([], [in_hbm(factor_two), in_hbm(factor_three)])
    if len(sizes) > 1:
        send([sent[0][0]])
    two = spread(factor_two, [sent[0][order.index(b)] for b in range(slabs, grid, slabs)], m, [sent[-1][-1]])
    three = [factor_three] + [sent[0][order.index(b)][-1, 0, :, ranks:] for b in range(1, slabs)]
    three = relative(jnp.concatenate(three), 1, fibs, fib).T
    high, low = split_outside(three)
    three = jnp.concatenate([high, high, low], axis=1)

    for c in range(len(sizes)):
        after = pieces[max(0, c - 1) * fibs:] if c < len(sizes) - 1 else pieces[max(0, c - 2) * fibs:(c - 1) * fibs]
        if c + 2 < len(sizes):
            send([sent[1][1 - c]])
            after = after + [sent[-1][-1]]
        shares = contract_two_three(sent[c], order, two, three, rows, slabs, fibs, after)
        pieces.append(shares[0])
        for b in range(1, fibs):
            pieces.append(partner(shares[b], "fib", fibs, b))

    def local_order(x):
        y = relative(x, 0, fibs, fib).reshape(fibs, il, ranks)
        starts = [sum(sizes[:c]) for c in range(len(sizes))]
        return jnp.concatenate([y[:, at:at + n].reshape(fibs * n, ranks) for at, n in zip(starts, sizes)])

    spots = [(a, sum(sizes[:c])) for c in range(len(sizes)) for a in range(fibs)]
    here = fib.reshape(1).astype(jnp.int32)
    target = gram_times(pieces, local_order(factor_one), here, spots)
    for axis, count in (("slab", slabs), ("row", rows), ("fib", fibs)):
        distance = 1
        while distance < count:
            target = target + partner(target, axis, count, distance)
            distance *= 2
    updated, ordered = orthonormal(target, here, spots)

    pairs = pieces[0].shape[1] // 2
    total = max(1, pairs // 4)
    pairs //= total
    got = []
    for n in range(total):
        parts = core_parts(pieces, ordered, me, n * pairs, pairs, grid)
        got.append([partner(parts[b], both, grid, b) if b else parts[b] for b in order])
    whole = []
    for n in range(total):
        whole = [assemble(got[n], order, me, ranks, n, total, whole)]
    return (updated, whole[0])


def solution(mesh):
    in_specs = (P("fib", "row", "slab", None), P(), P("row", None), P("slab", None), P())
    out_specs = (P(), P(None, ("row", "slab"), "fib", None))
    sizes = [mesh.shape[axis] for axis in ("fib", "row", "slab")]
    return jax.shard_map(
        functools.partial(body, *sizes), mesh=mesh, in_specs=in_specs, out_specs=out_specs, check_vma=False)
```

```python
import functools
import itertools

import jax
import jax.numpy as jnp
from jax import lax
from jax.experimental import pallas as pl
from jax.experimental.pallas import tpu as pltpu
from jax.sharding import PartitionSpec as P

F32 = jnp.float32
BF16 = jnp.bfloat16
HIGHEST = lax.Precision.HIGHEST
LANES = 128
TILE = 8
PIVOTS = 8
NT = (((1,), (1,)), ((), ()))
NN = (((1,), (0,)), ((), ()))


def split(x):
    high = x.astype(BF16)
    return high, (x - high.astype(F32)).astype(BF16)


def split_outside(x):
    high = lax.reduce_precision(x, 8, 7)
    return high.astype(BF16), (x - high).astype(BF16)


def dot(a, b, dims=NN):
    return lax.dot_general(a, b, dims, preferred_element_type=F32)


def relative(x, axis, count, me):
    shape = x.shape
    width = 1
    while width < count:
        cut = shape[:axis] + (count // (2 * width), 2, shape[axis] // count * width) + shape[axis + 1:]
        y = x.reshape(cut)
        x = jnp.where((me // width) % 2 == 1, jnp.flip(y, axis + 1), y).reshape(shape)
        width *= 2
    return x


def partner(x, axes, count, distance):
    return lax.ppermute(x, axes, [(s, s ^ distance) for s in range(count)])


def in_hbm(x):
    return pltpu.with_memory_space_constraint(x, pltpu.HBM)


def gathered(x, axes, count):
    return [x] + [partner(x, axes, count, b) for b in range(1, count)]


def params(steps, megabytes=12):
    return pltpu.CompilerParams(
        dimension_semantics=("arbitrary",) * steps, vmem_limit_bytes=megabytes * 2 ** 20
    )


def contract_four(tensor, factor, me, first, chunk, parts, after, riders, carriers):
    _, jl, kl, depth = tensor.shape
    ranks = factor.shape[0]
    m = LANES // jl
    groups = kl // m
    cuts = 1
    unit = 1 if riders else 2
    own = ranks // parts
    per = own // m
    steps = chunk + 1 if riders else chunk // unit
    last = chunk // unit - 1

    def kernel(me_ref, *refs):
        x_refs, f_ref, refs = refs[:cuts], refs[cuts], refs[cuts + 1:]
        outs, w_ref, s_ref = refs[len(after) + len(riders):-2], refs[-2], refs[-1]
        step = pl.program_id(0)

        @pl.when(step == 0)
        def _():
            high, low = split(f_ref[...])
            w_ref[...] = jnp.concatenate(
                [jnp.concatenate([high, high], 1), jnp.concatenate([low, jnp.zeros_like(low)], 1)], 0)

        if riders:
            @pl.when(step == chunk)
            def _():
                loads = jnp.concatenate([ref[...] for ref in refs[:len(riders)]], axis=1)
                for part in carriers:
                    outs[part][0] = jnp.zeros((per, kl, LANES), F32)
                    outs[part][0, 0] = loads

            @pl.when(step < chunk)
            def _():
                work(me_ref, x_refs, outs, w_ref, s_ref)
        else:
            work(me_ref, x_refs, outs, w_ref, s_ref)

    def work(me_ref, x_refs, outs, w_ref, s_ref):
        lane = lax.broadcasted_iota(jnp.int32, (1, 1, LANES), 2)
        weights = w_ref[...]
        for n in range(unit):
            for group in range(groups):
                rows = jnp.concatenate(
                    [x_ref[n, :, q * groups + group, :] for q in range(m) for x_ref in x_refs], axis=0)
                high, low = split(rows)
                found = dot(weights, jnp.concatenate([high, low], axis=1), NT)
                s_ref[n, :, group, :] = found[:ranks] + found[ranks:]
            for part in range(parts):
                mine = s_ref[n, pl.ds((me_ref[0] ^ part) * own, own)].reshape(per, m, groups, LANES)
                blocks = [mine[:, q] for q in range(m)]
                width = m // 2
                while width:
                    upper = (lane // (jl * width)) % 2 == 1
                    shift = jl * width
                    for q in range(m):
                        if q & width == 0:
                            a, b = blocks[q], blocks[q + width]
                            blocks[q] = jnp.where(upper, pltpu.roll(b, shift, 2), a)
                            blocks[q + width] = jnp.where(upper, b, pltpu.roll(a, LANES - shift, 2))
                    width //= 2
                for q in range(m):
                    outs[part][n, :, q * groups:(q + 1) * groups, :] = blocks[q]

    return pl.pallas_call(
        kernel,
        grid_spec=pltpu.PrefetchScalarGridSpec(
            num_scalar_prefetch=1,
            grid=(steps,),
            in_specs=[
                pl.BlockSpec(
                    (unit, jl // cuts, kl, depth),
                    lambda i, me, cut=cut: (first // unit + jnp.minimum(i, last), cut, 0, 0)) for cut in range(cuts)
            ] + [
                pl.BlockSpec(factor.shape, lambda i, me: (0, 0)),
            ] + [pl.BlockSpec(rider.shape, lambda i, me: (0, 0)) for rider in riders]
            + [pl.BlockSpec(memory_space=pl.ANY)] * len(after),
            out_specs=[
                pl.BlockSpec((1, per, kl, LANES), lambda i, me: (i, 0, 0, 0)) if riders and part in carriers else
                pl.BlockSpec((unit, per, kl, LANES), lambda i, me: (jnp.minimum(i, last), 0, 0, 0))
                for part in range(parts)],
            scratch_shapes=[
                pltpu.VMEM((2 * ranks, 2 * depth), BF16), pltpu.VMEM((unit, ranks, groups, LANES), F32)],
        ),
        out_shape=[
            jax.ShapeDtypeStruct((chunk + 1 if part in carriers else chunk, per, kl, LANES), F32)
            for part in range(parts)],
        compiler_params=params(1),
        cost_estimate=pl.CostEstimate(
            flops=12 * chunk * jl * kl * depth * ranks, bytes_accessed=6 * chunk * jl * kl * depth, transcendentals=0
        ),
        name="mode_four",
    )(me, *[tensor] * cuts, factor, *riders, *after)


def spread(own, carried, m, after):
    jl, ranks = own.shape
    count = 1 + len(carried)
    rows, wide = count * m * jl, m * ranks

    def kernel(*refs):
        out_ref = refs[-1]
        out_ref[...] = jnp.zeros_like(out_ref)
        for n, ref in enumerate(refs[:count]):
            for half, value in enumerate(split(ref[0, 0, :, :ranks] if n else ref[...])):
                for r in range(m):
                    at = (n * m + r) * jl
                    out_ref[at:at + jl, half * wide + r * ranks:half * wide + (r + 1) * ranks] = value

    return pl.pallas_call(
        kernel,
        grid=(1,),
        in_specs=[pl.BlockSpec((jl, ranks), lambda s: (0, 0))]
        + [pl.BlockSpec((1, 1, jl, LANES), lambda s, last=x.shape[0] - 1: (last, 0, 0, 0)) for x in carried]
        + [pl.BlockSpec(memory_space=pl.ANY)] * len(after),
        out_specs=pl.BlockSpec((rows, 2 * wide), lambda s: (0, 0)),
        out_shape=jax.ShapeDtypeStruct((rows, 2 * wide), BF16),
        compiler_params=params(1),
        name="spread",
    )(own, *carried, *after)


def contract_two_three(pieces, order, weights_two, weights_three, rows, slabs, targets, after):
    chunk, per, kl, _ = pieces[-1].shape
    wide = weights_two.shape[1] // 2
    ranks = weights_three.shape[0]
    share = ranks // targets
    count = len(pieces)

    def kernel(*refs):
        ins, two_ref, three_ref, outs = refs[:count], refs[count], refs[count + 1], refs[count + 2 + len(after):]
        taken = []
        for slab in range(slabs):
            taken.append(jnp.concatenate(
                [ins[order.index(row * slabs + slab)][...].reshape(chunk * kl, LANES) for row in range(rows)], axis=1))
        high, low = split(jnp.concatenate(taken, axis=0))
        two_high, two_low = two_ref[:, :wide], two_ref[:, wide:]
        half = dot(high, two_high) + dot(low, two_high) + dot(high, two_low)
        high, low = split(half)
        for i in range(chunk):
            spots = [slice((slab * chunk + i) * kl, (slab * chunk + i + 1) * kl) for slab in range(slabs)]
            own_high = jnp.concatenate([high[s] for s in spots], axis=0)
            own_low = jnp.concatenate([low[s] for s in spots], axis=0)
            full = dot(three_ref[...], jnp.concatenate([own_high, own_low, own_high], axis=0))
            for target in range(targets):
                outs[target][0, :, i, :] = full[target * share:(target + 1) * share]

    return pl.pallas_call(
        kernel,
        grid=(per,),
        in_specs=[pl.BlockSpec((chunk, 1, kl, LANES), lambda g: (0, g, 0, 0))] * count
        + [
            pl.BlockSpec(weights_two.shape, lambda g: (0, 0)),
            pl.BlockSpec(weights_three.shape, lambda g: (0, 0)),
        ] + [pl.BlockSpec(memory_space=pl.ANY)] * len(after),
        out_specs=[pl.BlockSpec((1, share, chunk, wide), lambda g: (g, 0, 0, 0))] * targets,
        out_shape=[jax.ShapeDtypeStruct((per, share, chunk, wide), F32)] * targets,
        compiler_params=params(1),
        cost_estimate=pl.CostEstimate(
            flops=6 * chunk * per * slabs * kl * (rows * LANES + ranks) * wide,
            bytes_accessed=8 * chunk * per * slabs * kl * rows * LANES,
            transcendentals=0,
        ),
        name="modes_two_three",
    )(*pieces, weights_two, weights_three, *after)


def gram_times(pieces, factor, fib, spots):
    per, share, _, wide = pieces[0].shape
    count = len(pieces)
    total = sum(piece.shape[2] for piece in pieces)
    block = min(share, 4)

    def kernel(fib_ref, *refs):
        ins, f_ref, out_ref, acc_ref = refs[:count], refs[count], refs[count + 1], refs[count + 2]
        step = pl.program_id(0)

        @pl.when(step == 0)
        def _():
            acc_ref[...] = jnp.zeros_like(acc_ref)

        found = None
        for g in range(per):
            for p in range(block):
                high, low = split(jnp.concatenate([ref[g, p] for ref in ins], axis=0))
                term = dot(high, jnp.concatenate([high, low], axis=0), NT)
                found = term if found is None else found + term
        acc_ref[...] += found

        @pl.when(step == pl.num_programs(0) - 1)
        def _():
            mixed = acc_ref[:, total:]
            gram = acc_ref[:, :total] + mixed + mixed.T
            target = lax.dot_general(gram, f_ref[...], NN, precision=HIGHEST, preferred_element_type=F32)
            for n, (group, spot) in enumerate(spots):
                at = pl.multiple_of((fib_ref[0] ^ group) * (total // fibs), TILE)
                out_ref[pl.ds(at + spot, TILE), :] = target[n * TILE:(n + 1) * TILE]

    fibs = 1 + max(group for group, _ in spots)
    return pl.pallas_call(
        kernel,
        grid_spec=pltpu.PrefetchScalarGridSpec(
            num_scalar_prefetch=1,
            grid=(share // block,),
            in_specs=[
                pl.BlockSpec((per, block, piece.shape[2], wide), lambda s, fib: (0, s, 0, 0)) for piece in pieces]
            + [pl.BlockSpec(factor.shape, lambda s, fib: (0, 0))],
            out_specs=pl.BlockSpec(factor.shape, lambda s, fib: (0, 0)),
            scratch_shapes=[pltpu.VMEM((total, 2 * total), F32)],
        ),
        out_shape=jax.ShapeDtypeStruct(factor.shape, F32),
        compiler_params=params(1),
        name="gram",
    )(fib, *pieces, factor)


def core_parts(pieces, updated, me, first, pairs, parts):
    per, _, _, wide = pieces[0].shape
    count = len(pieces)
    ranks = updated.shape[1]
    m = wide // ranks
    width = ranks // parts

    def kernel(me_ref, *refs):
        ins, u_ref, outs, t_ref, w_ref = refs[:count], refs[count], refs[count + 1:-2], refs[-2], refs[-1]

        @pl.when(pl.program_id(0) == 0)
        def _():
            high, low = split(u_ref[...].T)
            w_ref[...] = jnp.concatenate(
                [jnp.concatenate([high, high], 1), jnp.concatenate([low, jnp.zeros_like(low)], 1)], 0)

        for g in range(per):
            pair = []
            for p in range(2):
                high, low = split(jnp.concatenate([ref[g, p] for ref in ins], axis=0))
                found = dot(w_ref[...], jnp.concatenate([high, low], axis=0))
                pair.append(found[:ranks] + found[ranks:])
            t_ref[g] = jnp.concatenate(pair, axis=0).T.reshape(m, parts, width, 2 * ranks)
        for g in range(per):
            for part in range(parts):
                for r in range(m):
                    outs[part][0, g * m + r] = t_ref[g, r, me_ref[0] ^ part]

    shape = (pairs, per * m, width, 2 * ranks)
    return pl.pallas_call(
        kernel,
        grid_spec=pltpu.PrefetchScalarGridSpec(
            num_scalar_prefetch=1,
            grid=(pairs,),
            in_specs=[
                pl.BlockSpec((per, 2, piece.shape[2], wide), lambda s, me: (0, first + s, 0, 0)) for piece in pieces]
            + [pl.BlockSpec(updated.shape, lambda s, me: (0, 0))],
            out_specs=[pl.BlockSpec((1,) + shape[1:], lambda s, me: (s, 0, 0, 0))] * parts,
            scratch_shapes=[
                pltpu.VMEM((per, m, parts, width, 2 * ranks), F32),
                pltpu.VMEM((2 * ranks, 2 * updated.shape[0]), BF16)],
        ),
        out_shape=[jax.ShapeDtypeStruct(shape, F32)] * parts,
        compiler_params=params(1),
        name="core",
    )(me, *pieces, updated)


def assemble(parts, order, me, ranks, number, total, whole):
    pairs, own, width, lanes = parts[0].shape
    count = len(parts)

    def kernel(me_ref, *refs):
        ins, out_ref, s_ref = refs[:count], refs[-2], refs[-1]
        for pair in range(pairs):
            for ref, part in zip(ins, order):
                s_ref[pair, pl.ds((me_ref[0] ^ part) * own, own)] = ref[pair]
            for q in range(width):
                turned = s_ref[pair, :, q, :].T
                for p in range(2):
                    out_ref[:, q, 2 * pair + p, :] = turned[p * ranks:(p + 1) * ranks]

    return pl.pallas_call(
        kernel,
        grid_spec=pltpu.PrefetchScalarGridSpec(
            num_scalar_prefetch=1,
            grid=(1,),
            in_specs=[pl.BlockSpec((pairs, own, width, lanes), lambda s, me: (0, 0, 0, 0))] * count
            + [pl.BlockSpec(memory_space=pl.ANY)] * len(whole),
            out_specs=pl.BlockSpec((ranks, width, 2 * pairs, count * own), lambda s, me: (0, 0, number, 0)),
            scratch_shapes=[pltpu.VMEM((pairs, count * own, width, lanes), F32)],
        ),
        out_shape=jax.ShapeDtypeStruct((ranks, width, 2 * pairs * total, count * own), F32),
        input_output_aliases={1 + count: 0} if whole else {},
        compiler_params=params(1, 16),
        name="assemble",
    )(me, *parts, *whole)


def orthonormal(target, fib, spots):
    total, ranks = target.shape
    tile = 8

    fibs = 1 + max(group for group, _ in spots)

    def kernel(fib_ref, t_ref, out_ref, order_ref):
        z = t_ref[...]
        row = lax.broadcasted_iota(jnp.int32, (tile, 2 * ranks), 0)
        across = lax.broadcasted_iota(jnp.int32, (ranks, ranks), 1)
        down = lax.broadcasted_iota(jnp.int32, (ranks, ranks), 0)
        eye = jnp.where(across == down, jnp.float32(1), jnp.float32(0))
        for repeat in range(2):
            crossed = lax.dot_general(
                z, z, (((0,), (0,)), ((), ())), precision=HIGHEST, preferred_element_type=F32)
            whole = jnp.concatenate([crossed, eye], axis=1)
            blocks = [whole[b * tile:(b + 1) * tile] for b in range(ranks // tile)]
            for k in range(0, ranks, PIVOTS):
                home, spot = divmod(k, tile)
                columns = [
                    {b: jnp.broadcast_to(blocks[b][:, k + t:k + t + 1], (tile, 2 * ranks))
                     for b in range(home, len(blocks))} for t in range(PIVOTS)]
                tops = [blocks[home][spot + t:spot + t + 1] for t in range(PIVOTS)]
                for t in range(PIVOTS):
                    scale = lax.rsqrt(columns[t][home][spot + t:spot + t + 1])
                    tops[t] = tops[t] * scale
                    columns[t] = {b: column * scale for b, column in columns[t].items()}
                    for u in range(t + 1, PIVOTS):
                        side = columns[t][home][spot + u:spot + u + 1]
                        tops[u] = tops[u] - side * tops[t]
                        columns[u] = {b: column - side * columns[t][b] for b, column in columns[u].items()}
                for b in range(home, len(blocks)):
                    fresh = blocks[b]
                    for t in range(PIVOTS):
                        fresh = fresh - columns[t][b] * tops[t]
                    if b == home:
                        fresh = jnp.where(row >= spot + PIVOTS, fresh, blocks[b])
                        for t in range(PIVOTS):
                            fresh = jnp.where(row == spot + t, tops[t], fresh)
                    blocks[b] = fresh
            inverse = jnp.concatenate(blocks, axis=0)[:, ranks:]
            z = lax.dot_general(z, inverse, NT, precision=HIGHEST, preferred_element_type=F32)
        out_ref[...] = z
        for n, (group, spot) in enumerate(spots):
            at = pl.multiple_of((fib_ref[0] ^ group) * (total // fibs), TILE)
            order_ref[n * TILE:(n + 1) * TILE, :] = out_ref[pl.ds(at + spot, TILE), :]

    return pl.pallas_call(
        kernel,
        in_specs=[pl.BlockSpec(memory_space=pltpu.SMEM), pl.BlockSpec(memory_space=pltpu.VMEM)],
        out_specs=[pl.BlockSpec(memory_space=pltpu.VMEM)] * 2,
        out_shape=[jax.ShapeDtypeStruct(target.shape, F32)] * 2,
        compiler_params=params(0),
        name="orthonormal",
    )(fib, target)


def body(fibs, rows, slabs, tensor, factor_one, factor_two, factor_three, factor_four):
    both = ("row", "slab")
    grid = rows * slabs
    il, jl, _, _ = tensor.shape
    ranks = factor_four.shape[1]
    m = LANES // jl
    sizes = [TILE] * (il // TILE)
    fib = lax.axis_index("fib")
    place = lax.axis_index("row") * slabs + lax.axis_index("slab")
    me = place.reshape(1).astype(jnp.int32)

    tensor = in_hbm(tensor)
    far = list(range(grid // 2, grid))
    near = list(range(slabs, grid // 2)) + list(range(1, slabs))
    order = [b for pair in itertools.zip_longest(far, near) for b in pair if b is not None] + [0]
    sent, pieces = [], []

    carriers = [b for b in range(1, grid) if b < slabs or b % slabs == 0]

    def send(after, riders=()):
        c = len(sent)
        parts = contract_four(
            tensor, factor_four.T, me, sum(sizes[:c]), sizes[c], grid, after, riders, carriers if riders else ())
        sent.append([partner(parts[b], both, grid, b) if b else parts[b] for b in order])

    send([], [in_hbm(factor_two), in_hbm(factor_three)])
    if len(sizes) > 1:
        send([sent[0][0]])
    two = spread(factor_two, [sent[0][order.index(b)] for b in range(slabs, grid, slabs)], m, [sent[-1][-1]])
    three = [factor_three] + [sent[0][order.index(b)][-1, 0, :, ranks:] for b in range(1, slabs)]
    three = relative(jnp.concatenate(three), 1, fibs, fib).T
    high, low = split_outside(three)
    three = jnp.concatenate([high, high, low], axis=1)

    for c in range(len(sizes)):
        after = pieces[max(0, c - 1) * fibs:] if c < len(sizes) - 1 else pieces[max(0, c - 2) * fibs:(c - 1) * fibs]
        if c + 2 < len(sizes):
            send([sent[max(c, 1)][0]])
            after = after + [sent[-1][-1]]
        shares = contract_two_three(sent[c], order, two, three, rows, slabs, fibs, after)
        pieces.append(shares[0])
        for b in range(1, fibs):
            pieces.append(partner(shares[b], "fib", fibs, b))

    def local_order(x):
        y = relative(x, 0, fibs, fib).reshape(fibs, il, ranks)
        starts = [sum(sizes[:c]) for c in range(len(sizes))]
        return jnp.concatenate([y[:, at:at + n].reshape(fibs * n, ranks) for at, n in zip(starts, sizes)])

    spots = [(a, sum(sizes[:c])) for c in range(len(sizes)) for a in range(fibs)]
    here = fib.reshape(1).astype(jnp.int32)
    target = gram_times(pieces, local_order(factor_one), here, spots)
    for axis, count in (("slab", slabs), ("row", rows), ("fib", fibs)):
        distance = 1
        while distance < count:
            target = target + partner(target, axis, count, distance)
            distance *= 2
    updated, ordered = orthonormal(target, here, spots)

    pairs = pieces[0].shape[1] // 2
    total = max(1, pairs // 4)
    pairs //= total
    got = []
    for n in range(total):
        parts = core_parts(pieces, ordered, me, n * pairs, pairs, grid)
        got.append([partner(parts[b], both, grid, b) if b else parts[b] for b in order])
    whole = []
    for n in range(total):
        whole = [assemble(got[n], order, me, ranks, n, total, whole)]
    return (updated, whole[0])


def solution(mesh):
    in_specs = (P("fib", "row", "slab", None), P(), P("row", None), P("slab", None), P())
    out_specs = (P(), P(None, ("row", "slab"), "fib", None))
    sizes = [mesh.shape[axis] for axis in ("fib", "row", "slab")]
    return jax.shard_map(
        functools.partial(body, *sizes), mesh=mesh, in_specs=in_specs, out_specs=out_specs, check_vma=False)
```
